128 devices in a mesh: dp: 16 (over y, z), section: 2 (over x_hi), mp: 4 (over x_lo, core).
Axes of the slice: x: 4 (x_hi: 2, x_lo: 2; x = x_hi * 2 + x_lo), y: 4, z: 4, core: 2. Of those that a mesh axis runs over, the one named last changes fastest.
Arguments:
- tokens: bfloat16 [16384, 4096], P(('dp', 'section')), may hold values from -8 to 8
- routes: int32 [16384, 8], P(('dp', 'section')), may hold values from 0 to 127, all different within a row; in each aligned block of 512 rows (0 to 511, 512 to 1023, ...) at most 64 rows name the same one
- weight: bfloat16 [2, 16, 4096, 1536], P('section', 'dp', None, 'mp')
- quantized: bfloat16 [2, 16, 4096, 1536], P('section', 'dp', None, 'mp')
Outputs:
- refit_scale: float32 [2, 16, 1536], P('section', 'dp', 'mp')
- refit_bias: float32 [2, 16, 1536], P('section', 'dp', 'mp')
The draws below stay inside these ranges and needn't reach their ends.
Inputs may be any that keep to these rules, and one draw needn't show every extreme that they name: `routes`: each token names 8 different experts; the tokens of one device name any one expert at most 64 times.
All inputs are finite; a program needn't handle non-finite values.
Results may differ from the reference program's by a relative error of at most 0.0003.
Values may be sent and summed in bfloat16 or wider, within the bound.
A program may use at most 128 MiB of HBM per device.

```python
import math
import jax
import jax.numpy as jnp
import numpy as np
from jax import lax

D = 4096
F = 1536
EXPERTS = 128
TOP = 8
TOK_DEV = 512
PROJ = 2
CAP = 64
EXPERTS_WIN = 16
TOKENS = 16384
N_DP = 16
N_SECTION = 2


def shared_weight(key):
    base_draw = jax.random.normal(key, (PROJ, EXPERTS_WIN, D, F), jnp.float32)
    return jnp.clip(base_draw, -4.0, 4.0) * D ** (-0.5)


def draw_weight(key, part):
    base_draw = shared_weight(key)
    return base_draw.astype(jnp.bfloat16)


def draw_quantized(key, part):
    base_draw = shared_weight(key)
    key = jax.random.fold_in(key, 12)
    scale_key, noise_key = jax.random.split(key)
    column_scale = jnp.exp(jax.random.uniform(scale_key, (PROJ, EXPERTS_WIN, 1, F), jnp.float32, -0.6931, 0.6931))
    noise = 0.5 * jnp.clip(jax.random.normal(noise_key, (PROJ, EXPERTS_WIN, D, F), jnp.float32), -3.0, 3.0)
    return (base_draw * column_scale * (1.0 + noise)).astype(jnp.bfloat16)


def draw_tokens(key, part):
    key = jax.random.fold_in(key, 13)
    mean_key = jax.random.fold_in(key, 0)
    value_key = jax.random.fold_in(key, 2)
    feature_mean = 0.5 * jax.random.normal(mean_key, (1, D), jnp.float32)
    values = jax.random.normal(value_key, (TOKENS, D), jnp.float32)
    return jnp.clip(feature_mean + values, -8.0, 8.0).astype(jnp.bfloat16)


def routed_block(stream_key, own, number, rows, amount, top, most, lean):
    order = jax.random.permutation(stream_key, amount)
    crowded, common = shares(amount, rows * top, most, lean, True), shares(amount, rows * top, most, lean, False)
    places = jnp.arange(amount)

    def named(lengths, rotation):
        used = int((lengths > 0).sum())
        fixed = max(1, used // 4)
        passed = fixed + (places - fixed + rotation * (used - fixed)) % max(1, amount - fixed)
        return jnp.zeros((amount,), jnp.int32).at[order[jnp.where(places < fixed, places, passed)]].set(jnp.asarray(lengths, jnp.int32))

    lengths = jnp.where(number % 4 == 0, named(crowded, number // 4), named(common, number - number // 4 - 1))
    mixed = jax.random.permutation(jax.random.fold_in(own, 3), amount)
    donor, taker = mixed[0:amount // 2 * 2:2], mixed[1:amount // 2 * 2:2]
    margin = jnp.minimum(lengths[donor] - 1, most - lengths[taker]) // 2
    margin = jnp.where((donor == order[0]) | (taker == order[0]) | (lengths[taker] == 0), 0, jnp.maximum(margin, 0))
    passed = jax.random.randint(jax.random.fold_in(own, 4), (amount // 2,), 0, 1 << 20) % (margin + 1)
    lengths = lengths.at[donor].add(-passed).at[taker].add(passed)
    labels = jnp.searchsorted(jnp.cumsum(lengths), jnp.arange(rows * top), side="right").astype(jnp.int32)
    table = labels.reshape(top, rows).T
    table = table[jax.random.permutation(jax.random.fold_in(own, 1), rows)]
    rotation = jax.random.randint(jax.random.fold_in(own, 2), (rows, 1), 0, top)
    return jnp.take_along_axis(table, (jnp.arange(top)[None, :] + rotation) % top, axis=1)


def shares(number_of, total, most, lean, full):
    weights = [(1 << 20) // math.isqrt(grade ** lean) + 1 for grade in range(1, number_of + 1)]
    largest = most if full else min(most, max(-(-total // number_of), total * weights[0] // sum(weights)))
    least = 1 if total - largest >= number_of - 1 else 0
    given, spare = [largest] + [least] * (number_of - 1), total - largest - least * (number_of - 1)
    while spare > 0:
        candidates = [i for i in range(1, number_of) if given[i] < largest] or [i for i in range(1, number_of) if given[i] < most]
        pool, left = sum([weights[i] for i in candidates]), spare
        for i in candidates:
            more = min(most - given[i], max(1, left * weights[i] // pool), spare)
            given[i] = given[i] + more
            spare = spare - more
    return np.array(given)


def setup_inputs(seed: int = 0) -> dict:
    seeds = jax.random.split(jax.random.key(seed), 5)
    tokens = draw_tokens(jax.random.fold_in(seeds[4], 71), 0)
    routes_keys = jax.random.split(jax.random.fold_in(seeds[1], 1), TOKENS // TOK_DEV)
    routes_turns = jax.random.permutation(jax.random.fold_in(seeds[1], 3), TOKENS // TOK_DEV)
    routes = jax.vmap(lambda own, number: routed_block(jax.random.fold_in(seeds[1], 2), own, number, TOK_DEV, EXPERTS, TOP, CAP, 1))(routes_keys, routes_turns).reshape((TOKENS, TOP))
    weight = draw_weight(jax.random.fold_in(seeds[4], 71), 0)
    quantized = draw_quantized(jax.random.fold_in(seeds[4], 71), 0)
    return dict(tokens=tokens, routes=routes, weight=weight, quantized=quantized)


RIDGE = 1.0


def column_sums(row_block, weight_block, quant_block):
    full_out = jnp.dot(row_block, weight_block, preferred_element_type=jnp.float32)
    quant_out = jnp.dot(row_block, quant_block, preferred_element_type=jnp.float32)
    return jnp.stack([
        jnp.sum(quant_out * quant_out, axis=0),
        jnp.sum(quant_out, axis=0),
        jnp.sum(quant_out * full_out, axis=0),
        jnp.sum(full_out, axis=0)])


def refit_columns(moments, counts):
    square = moments[0]
    first_moment = moments[1]
    cross_term = moments[2]
    target = moments[3]
    denominator = counts + RIDGE
    diagonal = square + RIDGE
    anchored = cross_term + RIDGE
    determinant = diagonal * denominator - first_moment * first_moment
    refit_scale = (denominator * anchored - first_moment * target) / determinant
    refit_bias = (diagonal * target - first_moment * anchored) / determinant
    return refit_scale, refit_bias


def reference(tokens, routes, weight, quantized):
    capacity_rows = N_DP * N_SECTION * CAP

    def one_expert(expert):
        member = jnp.any(routes == expert, axis=1)
        counts = jnp.sum(member.astype(jnp.int32))
        row_index = jnp.nonzero(member, size=capacity_rows, fill_value=0)[0].astype(jnp.int32)
        present = jnp.arange(capacity_rows, dtype=jnp.int32) < counts
        row_block = jnp.where(present[:, None], tokens[row_index], jnp.zeros((), tokens.dtype))
        moments = jnp.stack([column_sums(row_block, weight[proj_index, expert], quantized[proj_index, expert])
                             for proj_index in range(PROJ)], axis=1)
        return moments, counts

    moments, counts = lax.map(one_expert, jnp.arange(EXPERTS_WIN, dtype=jnp.int32))
    moments = jnp.transpose(moments, (1, 2, 0, 3))
    counts = counts.astype(jnp.float32)[None, :, None]
    refit_scale, refit_bias = refit_columns(moments, counts)
    return refit_scale, refit_bias
```

```python
import functools

import jax
import jax.numpy as jnp
from jax import lax
from jax.experimental import pallas as pl
from jax.experimental.pallas import tpu as pltpu
from jax.sharding import PartitionSpec as P

CAP = 64
RIDGE = 1.0
MESH = pl.DeviceIdType.MESH
SIDE = 4
SHIFTS = SIDE * SIDE
GROUP = SIDE * CAP


def kernel(
    tok_hbm,
    routes_ref,
    w_hbm,
    q_hbm,
    scale_ref,
    bias_ref,
    tok,
    wq,
    outbox,
    rows,
    places,
    acc,
    mom,
    tally,
    tally_in,
    tally_other,
    load_sem,
    a_send,
    a_recv,
    x_send,
    x_recv,
    f_send,
    f_recv,
    c_send,
    c_recv,
    d_send,
    d_recv,
    t_send,
    t_recv,
    u_sem,
):
    dp, section, mp = lax.axis_index("dp"), lax.axis_index("section"), lax.axis_index("mp")
    y, z = dp // SIDE, dp % SIDE
    x_lo, core = mp // 2, mp % 2
    half = tok.shape[1]
    token_total = tok.shape[0]
    columns = w_hbm.shape[-1]

    across = (dp, 1 - section, (1 - x_lo) * 2 + core)
    beside = (dp, section, (1 - x_lo) * 2 + core)
    twin = (dp, section, x_lo * 2 + 1 - core)
    mine = jnp.where(section == x_lo, 0, CAP // 2)
    theirs = CAP // 2 - mine

    def shift(k):
        dy = k % SIDE
        dz = (k // SIDE + k) % SIDE
        return ((y + dy) % SIDE) * SIDE + (z + dz) % SIDE

    def rows_at(region, k, start=0, size=CAP):
        first = pl.multiple_of((region * SHIFTS + k) * CAP + start, 16)
        return pl.ds(first, size)

    def a_copy(k):
        return pltpu.make_async_remote_copy(
            outbox.at[pl.ds(pl.multiple_of(k * CAP, CAP), CAP)],
            rows.at[core, rows_at(0, k)],
            a_send.at[k],
            a_recv.at[k],
            (shift(k), section, mp),
            MESH,
        )

    def t_copy(k):
        return pltpu.make_async_remote_copy(
            tally, tally_in.at[k], t_send.at[k], t_recv.at[k], (shift(k), section, mp), MESH
        )

    def x_copy(k):
        return pltpu.make_async_remote_copy(
            rows.at[core, rows_at(0, k, mine, CAP // 2)],
            rows.at[core, rows_at(1, k, mine, CAP // 2)],
            x_send.at[k],
            x_recv.at[k],
            across,
            MESH,
        )

    def f_copy(k, start):
        return pltpu.make_async_remote_copy(
            rows.at[core, rows_at(1, k, start, CAP // 2)],
            rows.at[core, rows_at(1, k, start, CAP // 2)],
            f_send.at[k],
            f_recv.at[k],
            beside,
            MESH,
        )

    def c_copy(k, owner):
        return pltpu.make_async_remote_copy(
            rows.at[owner, rows_at(0, k)],
            rows.at[owner, rows_at(0, k)],
            c_send.at[k],
            c_recv.at[k],
            twin,
            MESH,
        )

    def d_copy(k, owner):
        return pltpu.make_async_remote_copy(
            rows.at[owner, rows_at(1, k)],
            rows.at[owner, rows_at(1, k)],
            d_send.at[k],
            d_recv.at[k],
            twin,
            MESH,
        )

    loads = [
        pltpu.make_async_copy(
            tok_hbm.at[:, pl.ds(pl.multiple_of(core * half, half), half)], tok, load_sem.at[0]
        )
    ]
    for part in range(2):
        for i, source in enumerate((w_hbm, q_hbm)):
            loads.append(
                pltpu.make_async_copy(
                    source.at[0, 0, pl.ds(part * half, half)],
                    wq.at[part, :, pl.ds(i * columns, columns)],
                    load_sem.at[1 + 2 * part + i],
                )
            )
    for load in loads:
        load.start()

    barrier = pltpu.get_barrier_semaphore()
    for k in range(1, SHIFTS):
        pl.semaphore_signal(barrier, 1, device_id=(shift(k), section, mp), device_id_type=MESH)
    for peer in (across, beside, twin):
        pl.semaphore_signal(barrier, 1, device_id=peer, device_id_type=MESH)

    lanes = lax.broadcasted_iota(jnp.int32, (token_total, 128), 1)
    chosen = jnp.zeros((token_total, 128), jnp.float32)
    for i in range(routes_ref.shape[1]):
        chosen += jnp.where(routes_ref[:, i : i + 1] == lanes, 1.0, 0.0)
    before = lax.broadcasted_iota(jnp.int32, (token_total, token_total), 1)
    after = lax.broadcasted_iota(jnp.int32, (token_total, token_total), 0)
    lower = jnp.where(before <= after, 1.0, 0.0).astype(jnp.bfloat16)
    rank = jnp.dot(lower, chosen.astype(jnp.bfloat16), preferred_element_type=jnp.float32)
    tally[...] = jnp.broadcast_to(rank[token_total - 1 :], tally.shape)
    place = jnp.where(chosen > 0, rank - 1.0, -1.0)
    places[...] = jnp.transpose(place)
    mom[...] = jnp.zeros_like(mom)
    loads[0].wait()

    slot = lax.broadcasted_iota(jnp.int32, (CAP, token_total), 0).astype(jnp.float32)

    def collect(group):
        picks = []
        for j in range(SIDE):
            k = group * SIDE + j
            line = places[pl.ds(shift(k), 1), :]
            picks.append(jnp.where(line == slot, 1.0, 0.0).astype(jnp.bfloat16))
        pick = jnp.concatenate(picks, axis=0)
        first = pl.multiple_of(group * GROUP, GROUP)
        outbox[pl.ds(first, GROUP), :] = jnp.dot(
            pick, tok[...], preferred_element_type=jnp.float32
        ).astype(jnp.bfloat16)

    collect(0)
    rows[core, :CAP, :] = outbox[:CAP, :]
    pl.semaphore_wait(barrier, SHIFTS + 2)

    for k in range(1, SIDE):
        a_copy(k).start()
    x_copy(0).start()
    c_copy(0, core).start()
    for k in range(1, SHIFTS):
        t_copy(k).start()

    @pl.loop(1, SIDE)
    def _(group):
        collect(group)
        for j in range(SIDE):
            a_copy(group * SIDE + j).start()

    for load in loads[1:]:
        load.wait()

    def multiply(region, group):
        first = pl.multiple_of((region * SHIFTS + group * SIDE) * CAP, GROUP)
        acc[...] = jnp.dot(
            rows[0, pl.ds(first, GROUP), :], wq[0], preferred_element_type=jnp.float32
        ) + jnp.dot(rows[1, pl.ds(first, GROUP), :], wq[1], preferred_element_type=jnp.float32)
        full = acc[:, :columns]
        quant = acc[:, columns:]

        def fold(values):
            return jnp.sum(values.reshape(GROUP // 8, 8, columns), axis=0)

        mom[0] += fold(quant * quant)
        mom[1] += fold(quant)
        mom[2] += fold(quant * full)
        mom[3] += fold(full)

    def finish_own(group):
        for j in range(SIDE):
            c_copy(group * SIDE + j, 1 - core).wait_recv()
        multiply(0, group)

    def finish_other(group):
        for j in range(SIDE):
            d_copy(group * SIDE + j, 1 - core).wait_recv()
        multiply(1, group)

    def arrive(k):
        a_copy(k).wait_recv()
        x_copy(k).start()
        c_copy(k, core).start()

    def relay(k):
        x_copy(k).wait_recv()
        f_copy(k, mine).start()

    def hand(k):
        f_copy(k, theirs).wait_recv()
        d_copy(k, core).start()

    @pl.loop(0, SIDE)
    def _(group):
        for j in range(SIDE):
            k = group * SIDE + j
            if j:
                arrive(k)
                relay(k - 1)
                if j > 1:
                    hand(k - 2)
                else:
                    pl.when(group > 0)(lambda: hand(k - 2))
            else:

                @pl.when(group > 0)
                def _():
                    arrive(k)
                    relay(k - 1)
                    hand(k - 2)

        pl.when(group > 0)(lambda: finish_own(group - 1))
        pl.when(group > 1)(lambda: finish_other(group - 2))

    last = SHIFTS - 1
    relay(last)
    hand(last - 1)
    finish_own(SIDE - 1)
    hand(last)
    finish_other(SIDE - 2)

    total = tally[...]
    for k in range(1, SHIFTS):
        t_copy(k).wait_recv()
        total += tally_in[k]
    tally_in[0] = total
    u_copy = pltpu.make_async_remote_copy(
        tally_in.at[0], tally_other, u_sem.at[0], u_sem.at[1], across, MESH
    )
    u_copy.start()

    finish_other(SIDE - 1)

    u_copy.wait()
    total += tally_other[...]
    lane = lax.broadcasted_iota(jnp.int32, total.shape, 1)
    counts = jnp.sum(jnp.where(lane == dp, total, 0.0), axis=1, keepdims=True)[:1]

    square, first_moment, cross_term, target = (
        jnp.sum(mom[i], axis=0, keepdims=True) for i in range(4)
    )
    denominator = counts + RIDGE
    diagonal = square + RIDGE
    anchored = cross_term + RIDGE
    determinant = diagonal * denominator - first_moment * first_moment
    scale_ref[0] = (denominator * anchored - first_moment * target) / determinant
    bias_ref[0] = (diagonal * target - first_moment * anchored) / determinant

    @pl.loop(1, SHIFTS)
    def _(k):
        a_copy(k).wait_send()
        t_copy(k).wait_send()

    @pl.loop(0, SHIFTS)
    def _(k):
        x_copy(k).wait_send()
        f_copy(k, mine).wait_send()
        c_copy(k, core).wait_send()
        d_copy(k, core).wait_send()


def local(tokens, routes, weight, quantized):
    token_total, width = tokens.shape
    columns = weight.shape[-1]
    out = jax.ShapeDtypeStruct((1, 1, columns), jnp.float32)
    vmem = pl.BlockSpec(memory_space=pltpu.VMEM)
    hbm = pl.BlockSpec(memory_space=pl.ANY)
    sems = pltpu.SemaphoreType.DMA
    return pl.pallas_call(
        kernel,
        out_shape=(out, out),
        in_specs=[hbm, vmem, hbm, hbm],
        out_specs=(vmem, vmem),
        scratch_shapes=[
            pltpu.VMEM((token_total, width // 2), jnp.bfloat16),
            pltpu.VMEM((2, width // 2, 2 * columns), jnp.bfloat16),
            pltpu.VMEM((SHIFTS * CAP, width // 2), jnp.bfloat16),
            pltpu.VMEM((2, 2 * SHIFTS * CAP, width // 2), jnp.bfloat16),
            pltpu.VMEM((128, token_total), jnp.float32),
            pltpu.VMEM((GROUP, 2 * columns), jnp.float32),
            pltpu.VMEM((4, 8, columns), jnp.float32),
            pltpu.VMEM((8, 128), jnp.float32),
            pltpu.VMEM((SHIFTS, 8, 128), jnp.float32),
            pltpu.VMEM((8, 128), jnp.float32),
            sems((5,)),
        ]
        + [sems((SHIFTS,))] * 12
        + [sems((2,))],
        compiler_params=pltpu.CompilerParams(
            collective_id=0, has_side_effects=True, vmem_limit_bytes=56 << 20
        ),
        cost_estimate=pl.CostEstimate(
            flops=2 * 2048 * 4096 * 768, bytes_accessed=10 << 20, transcendentals=0
        ),
    )(tokens, routes, weight, quantized)


def solution(mesh):
    placed = (
        P(("dp", "section"), None),
        P(("dp", "section"), None),
        P("section", "dp", None, "mp"),
        P("section", "dp", None, "mp"),
    )
    return jax.shard_map(
        local,
        mesh=mesh,
        in_specs=placed,
        out_specs=(P("section", "dp", "mp"), P("section", "dp", "mp")),
        check_vma=False,
    )
```

```python
import functools

import jax
import jax.numpy as jnp
from jax import lax
from jax.experimental import pallas as pl
from jax.experimental.pallas import tpu as pltpu
from jax.sharding import PartitionSpec as P

CAP = 64
RIDGE = 1.0
MESH = pl.DeviceIdType.MESH
SIDE = 4
SHIFTS = SIDE * SIDE
PIECE = CAP // 2
UNIT = PIECE // 2
GROUP = SIDE * PIECE
PRODUCTS = {
    2: (0,), 5: (8,), 6: (1,), 7: (12,), 9: (9,), 10: (2,), 11: (13,), 12: (4,), 13: (10,),
    14: (3, 5), 15: (14,), 16: (6,), 17: (11, 7), 18: (15,),
}
STEPS = 19
NEAREST = (
    (0, 0), (1, 0), (0, 1), (3, 0), (0, 3), (1, 1), (3, 3), (1, 3),
    (3, 1), (2, 0), (0, 2), (1, 2), (3, 2), (2, 1), (2, 3), (2, 2),
)
EARLY = 2
REST = 9
AHEAD = 8
RELAY_LAG = 1
HAND_LAG = 2
SENT_LAG = 4


def kernel(
    tok_hbm,
    routes_hbm,
    w_hbm,
    q_hbm,
    out_ref,
    routes,
    tok,
    wq,
    outbox,
    rows,
    places,
    acc,
    mom,
    tally,
    tally_in,
    tally_other,
    load_sem,
    a_send,
    a_recv,
    x_send,
    x_recv,
    f_send,
    f_recv,
    c_send,
    c_recv,
    t_send,
    t_recv,
    u_sem,
):
    dp, section, mp = lax.axis_index("dp"), lax.axis_index("section"), lax.axis_index("mp")
    y, z = dp // SIDE, dp % SIDE
    x_lo, core = mp // 2, mp % 2
    half = tok.shape[1]
    token_total = tok.shape[0]
    columns = w_hbm.shape[-1]

    across = (dp, 1 - section, (1 - x_lo) * 2 + core)
    beside = (dp, section, (1 - x_lo) * 2 + core)
    twin = (dp, section, x_lo * 2 + 1 - core)
    mine = jnp.where(section == x_lo, 0, PIECE)

    def shift(k):
        code = 0
        for i, (dy, dz) in enumerate(NEAREST):
            code = jnp.where(k % SHIFTS == i, dy * SIDE + dz, code)
        return ((y + code // SIDE) % SIDE) * SIDE + (z + code % SIDE) % SIDE

    def span(index, size):
        return pl.ds(pl.multiple_of(index * size, size), size)

    def remote(source, target, send, recv, device):
        return pltpu.make_async_remote_copy(source, target, send, recv, device, MESH)

    def a_copy(p):
        return remote(
            outbox.at[span(p, PIECE)],
            rows.at[core, span(p, PIECE)],
            a_send.at[p],
            a_recv.at[p],
            (shift(p), section, mp),
        )

    def t_copy(k):
        return remote(tally, tally_in.at[k], t_send.at[k], t_recv.at[k], (shift(k), section, mp))

    def u_copy():
        return remote(tally_in.at[0], tally_other, u_sem.at[0], u_sem.at[1], across)

    units = SHIFTS * PIECE // UNIT

    def x_copy(u):
        return remote(
            rows.at[core, span(u, UNIT)],
            rows.at[core, span(2 * units + u, UNIT)],
            x_send.at[u],
            x_recv.at[u],
            across,
        )

    def f_copy(u):
        return remote(
            rows.at[core, span(2 * units + u, UNIT)],
            rows.at[core, span(3 * units + u, UNIT)],
            f_send.at[u],
            f_recv.at[u],
            beside,
        )

    def c_copy(p, owner):
        return remote(
            rows.at[owner, span(p, PIECE)],
            rows.at[owner, span(p, PIECE)],
            c_send.at[p],
            c_recv.at[p],
            twin,
        )

    load_routes = pltpu.make_async_copy(routes_hbm, routes, load_sem.at[5])
    load_tok = pltpu.make_async_copy(
        tok_hbm.at[:, pl.ds(pl.multiple_of(core * half, half), half)], tok, load_sem.at[0]
    )
    loads = []
    for part in range(2):
        for i, source in enumerate((w_hbm, q_hbm)):
            loads.append(
                pltpu.make_async_copy(
                    source.at[0, 0, pl.ds(part * half, half)],
                    wq.at[part, :, pl.ds(i * columns, columns)],
                    load_sem.at[1 + 2 * part + i],
                )
            )
    load_routes.start()
    load_tok.start()

    barrier = pltpu.get_barrier_semaphore()
    for k in range(1, SHIFTS):
        pl.semaphore_signal(barrier, 1, device_id=(shift(k), section, mp), device_id_type=MESH)
    for peer in (across, beside, twin):
        pl.semaphore_signal(barrier, 1, device_id=peer, device_id_type=MESH)

    expert = lax.broadcasted_iota(jnp.int32, (SHIFTS, token_total), 0)
    before = lax.broadcasted_iota(jnp.int32, (token_total, token_total), 0)
    after = lax.broadcasted_iota(jnp.int32, (token_total, token_total), 1)
    upper = jnp.where(before <= after, 1.0, 0.0).astype(jnp.bfloat16)
    mom[...] = jnp.zeros_like(mom)
    load_routes.wait()
    chosen = jnp.zeros((SHIFTS, token_total), jnp.float32)
    for i in range(routes.shape[0]):
        chosen += jnp.where(routes[i : i + 1, :] == expert, 1.0, 0.0)
    rank = jnp.dot(chosen.astype(jnp.bfloat16), upper, preferred_element_type=jnp.float32)
    places[...] = jnp.where(chosen > 0, rank - 1.0, -1.0)
    tally[...] = jnp.broadcast_to(jnp.sum(chosen, axis=1, keepdims=True), tally.shape)
    load_tok.wait()

    slot = lax.broadcasted_iota(jnp.int32, (PIECE, token_total), 0)

    def collect(group):
        start = jnp.where(group < SIDE, mine, PIECE - mine)
        number = (slot + start).astype(jnp.float32)
        picks = []
        for j in range(SIDE):
            line = places[pl.ds(shift(group * SIDE + j), 1), :]
            picks.append(jnp.where(line == number, 1.0, 0.0).astype(jnp.bfloat16))
        pick = jnp.concatenate(picks, axis=0)
        outbox[span(group, GROUP), :] = jnp.dot(
            pick, tok[...], preferred_element_type=jnp.float32
        ).astype(jnp.bfloat16)

    def launch(p, ready):
        @pl.when(ready & (p % SHIFTS > 0) & (p < 2 * SHIFTS))
        def _():
            a_copy(p).start()

    def own_piece(p):
        rows[core, span(p, PIECE), :] = outbox[span(p, PIECE), :]

    def carry(p):
        for i in range(2):
            x_copy(2 * p + i).start()

    collect(0)
    pl.semaphore_wait(barrier, SHIFTS + 2)
    for p in range(1, SIDE):
        a_copy(p).start()
    own_piece(0)
    carry(0)
    c_copy(0, core).start()

    @pl.loop(1, 2 * SIDE)
    def _(group):
        collect(group)
        for j in range(SIDE):

            launch(group * SIDE + j, group * SIDE + j < AHEAD)

    own_piece(SHIFTS)
    c_copy(SHIFTS, core).start()
    for load in loads:
        load.start()
    for k in range(1, SHIFTS):
        t_copy(k).start()
    for load in loads:
        load.wait()

    def multiply(group):
        for j in range(SIDE):
            c_copy(group * SIDE + j, 1 - core).wait_recv()
        acc[...] = jnp.dot(
            rows[0, span(group, GROUP), :], wq[0], preferred_element_type=jnp.float32
        ) + jnp.dot(rows[1, span(group, GROUP), :], wq[1], preferred_element_type=jnp.float32)
        full = acc[:, :columns]
        quant = acc[:, columns:]

        def fold(values):
            return jnp.sum(values.reshape(GROUP // 8, 8, columns), axis=0)

        mom[0] += fold(quant * quant)
        mom[1] += fold(quant)
        mom[2] += fold(quant * full)
        mom[3] += fold(full)

    def sent(k):
        for p in (2 * k, 2 * k + 1):

            @pl.when(p % SHIFTS > 0)
            def _():
                a_copy(p).wait_send()

            x_copy(p).wait_send()
            f_copy(p).wait_send()
        c_copy(k, core).wait_send()
        c_copy(2 * SHIFTS + k, core).wait_send()
        c_copy(3 * SHIFTS + k, core).wait_send()

    def arrive(p):
        a_copy(p).wait_recv()
        carry(p)
        c_copy(p, core).start()

    for p in range(1, EARLY + 1):
        arrive(p)

    @pl.loop(0, STEPS)
    def _(step):
        for j in range(2):
            launch(AHEAD + 2 * step + j, True)

        @pl.when((step > 0) & (step + EARLY < SHIFTS))
        def _():
            arrive(step + EARLY)

        @pl.when((step >= RELAY_LAG) & (step < SHIFTS + RELAY_LAG))
        def _():
            k = step - RELAY_LAG
            for i in range(2):
                x_copy(2 * k + i).wait_recv()
                f_copy(2 * k + i).start()
            c_copy(2 * SHIFTS + k, core).start()

        @pl.when((step >= HAND_LAG) & (step < SHIFTS + HAND_LAG))
        def _():
            k = step - HAND_LAG
            for i in range(2):
                f_copy(2 * k + i).wait_recv()
            c_copy(3 * SHIFTS + k, core).start()

        @pl.when((step >= REST) & (step < REST + SHIFTS // 2))
        def _():
            for j in range(2):
                p = SHIFTS + 2 * (step - REST) + j

                @pl.when(p > SHIFTS)
                def _():
                    a_copy(p).wait_recv()
                    c_copy(p, core).start()

        for i in range(2):
            group = -1
            for at, groups in PRODUCTS.items():
                if len(groups) > i:
                    group = jnp.where(step == at, groups[i], group)
            pl.when(group >= 0)(functools.partial(multiply, group))

        @pl.when((step >= SENT_LAG) & (step < SHIFTS))
        def _():
            sent(step - SENT_LAG)

        @pl.when(step == SHIFTS // 2)
        def _():
            total = tally[...]
            for k in range(1, SHIFTS):
                t_copy(k).wait()
                total += tally_in[k]
            tally_in[0] = total
            u_copy().start()

    u_copy().wait()
    total = tally_in[0] + tally_other[...]
    named = lax.broadcasted_iota(jnp.int32, total.shape, 0)
    counts = jnp.sum(jnp.where(named == dp, total, 0.0), axis=0, keepdims=True)[:, :1]
    for i in range(4):
        out_ref[i : i + 1, :] = jnp.sum(mom[i], axis=0, keepdims=True)
    out_ref[4:, :] = jnp.broadcast_to(counts, (4, columns))

    for k in range(SHIFTS - SENT_LAG, SHIFTS):
        sent(k)
    for k in range(SHIFTS):
        c_copy(SHIFTS + k, core).wait_send()


def refit_columns(sums):
    square, first_moment, cross_term, target, counts = (sums[i] for i in range(5))
    denominator = counts + RIDGE
    diagonal = square + RIDGE
    anchored = cross_term + RIDGE
    determinant = diagonal * denominator - first_moment * first_moment
    refit_scale = (denominator * anchored - first_moment * target) / determinant
    refit_bias = (diagonal * target - first_moment * anchored) / determinant
    return refit_scale[None, None], refit_bias[None, None]


def local(tokens, routes, weight, quantized):
    token_total, width = tokens.shape
    columns = weight.shape[-1]
    vmem = pl.BlockSpec(memory_space=pltpu.VMEM)
    hbm = pl.BlockSpec(memory_space=pl.ANY)
    sems = pltpu.SemaphoreType.DMA
    sums = pl.pallas_call(
        kernel,
        out_shape=jax.ShapeDtypeStruct((8, columns), jnp.float32),
        in_specs=[hbm, hbm, hbm, hbm],
        out_specs=vmem,
        scratch_shapes=[
            pltpu.VMEM(routes.T.shape, jnp.int32),
            pltpu.VMEM((token_total, width // 2), jnp.bfloat16),
            pltpu.VMEM((2, width // 2, 2 * columns), jnp.bfloat16),
            pltpu.VMEM((SHIFTS * CAP, width // 2), jnp.bfloat16),
            pltpu.VMEM((2, 2 * SHIFTS * CAP, width // 2), jnp.bfloat16),
            pltpu.VMEM((SHIFTS, token_total), jnp.float32),
            pltpu.VMEM((GROUP, 2 * columns), jnp.float32),
            pltpu.VMEM((4, 8, columns), jnp.float32),
            pltpu.VMEM((SHIFTS, 128), jnp.float32),
            pltpu.VMEM((SHIFTS, SHIFTS, 128), jnp.float32),
            pltpu.VMEM((SHIFTS, 128), jnp.float32),
            sems((6,)),
        ]
        + [sems((2 * SHIFTS,))] * 6
        + [sems((4 * SHIFTS,))] * 2
        + [sems((SHIFTS,))] * 2
        + [sems((2,))],
        compiler_params=pltpu.CompilerParams(
            collective_id=0, has_side_effects=True, vmem_limit_bytes=56 << 20
        ),
        cost_estimate=pl.CostEstimate(
            flops=2 * 2048 * 4096 * 768, bytes_accessed=10 << 20, transcendentals=0
        ),
    )(tokens, routes.T, weight, quantized)
    return refit_columns(sums)


def solution(mesh):
    placed = (
        P(("dp", "section"), None),
        P(("dp", "section"), None),
        P("section", "dp", None, "mp"),
        P("section", "dp", None, "mp"),
    )
    return jax.shard_map(
        local,
        mesh=mesh,
        in_specs=placed,
        out_specs=(P("section", "dp", "mp"), P("section", "dp", "mp")),
        check_vma=False,
    )
```

```python
import functools

import jax
import jax.numpy as jnp
from jax import lax
from jax.experimental import pallas as pl
from jax.experimental.pallas import tpu as pltpu
from jax.sharding import PartitionSpec as P

CAP = 64
RIDGE = 1.0
MESH = pl.DeviceIdType.MESH
SIDE = 4
SHIFTS = SIDE * SIDE
PIECE = CAP // 2
UNIT = PIECE // 2
GROUP = SIDE * PIECE
PRODUCTS = {
    2: (0,), 5: (8,), 6: (1,), 8: (12,), 9: (9,), 10: (2,), 11: (13,), 13: (10, 4),
    14: (3,), 15: (5,), 16: (14,), 17: (6, 11), 19: (15, 7),
}
STEPS = 20
NEAREST = (
    (0, 0), (1, 0), (0, 1), (3, 0), (0, 3), (1, 1), (3, 3), (1, 3),
    (3, 1), (2, 0), (0, 2), (1, 2), (2, 1), (3, 2), (2, 3), (2, 2),
)
SHIFT_ORDER = NEAREST + NEAREST
EARLY = 2
REST = 11
AHEAD = 8
STEPS_SEND = (2 * SHIFTS - AHEAD) // 2
RELAY_LAG = 1
HAND_LAG = 3
SENT_LAG = 5


def kernel(
    tok_hbm,
    routes_hbm,
    w_hbm,
    q_hbm,
    out_ref,
    routes,
    tok,
    wq,
    outbox,
    rows,
    places,
    acc,
    mom,
    tally,
    tally_in,
    tally_other,
    load_sem,
    a_send,
    a_recv,
    x_send,
    x_recv,
    f_send,
    f_recv,
    c_send,
    c_recv,
    t_send,
    t_recv,
    u_sem,
):
    dp, section, mp = lax.axis_index("dp"), lax.axis_index("section"), lax.axis_index("mp")
    y, z = dp // SIDE, dp % SIDE
    x_lo, core = mp // 2, mp % 2
    half = tok.shape[1]
    token_total = tok.shape[0]
    columns = w_hbm.shape[-1]

    across = (dp, 1 - section, (1 - x_lo) * 2 + core)
    beside = (dp, section, (1 - x_lo) * 2 + core)
    twin = (dp, section, x_lo * 2 + 1 - core)
    mine = jnp.where(section == x_lo, 0, PIECE)

    def shift(k):
        code = 0
        for i, (dy, dz) in enumerate(SHIFT_ORDER):
            code = jnp.where(k == i, dy * SIDE + dz, code)
        return ((y + code // SIDE) % SIDE) * SIDE + (z + code % SIDE) % SIDE

    def span(index, size):
        return pl.ds(pl.multiple_of(index * size, size), size)

    def remote(source, target, send, recv, device):
        return pltpu.make_async_remote_copy(source, target, send, recv, device, MESH)

    def a_copy(p):
        return remote(
            outbox.at[span(p, PIECE)],
            rows.at[core, span(p, PIECE)],
            a_send.at[p],
            a_recv.at[p],
            (shift(p), section, mp),
        )

    def t_copy(k):
        return remote(tally, tally_in.at[k], t_send.at[k], t_recv.at[k], (shift(k), section, mp))

    def u_copy():
        return remote(tally_in.at[0], tally_other, u_sem.at[0], u_sem.at[1], across)

    units = SHIFTS * PIECE // UNIT

    def x_copy(u):
        return remote(
            rows.at[core, span(u, UNIT)],
            rows.at[core, span(2 * units + u, UNIT)],
            x_send.at[u],
            x_recv.at[u],
            across,
        )

    def f_copy(u):
        return remote(
            rows.at[core, span(2 * units + u, UNIT)],
            rows.at[core, span(3 * units + u, UNIT)],
            f_send.at[u],
            f_recv.at[u],
            beside,
        )

    def c_copy(p, owner):
        return remote(
            rows.at[owner, span(p, PIECE)],
            rows.at[owner, span(p, PIECE)],
            c_send.at[p],
            c_recv.at[p],
            twin,
        )

    load_routes = pltpu.make_async_copy(routes_hbm, routes, load_sem.at[5])
    load_tok = pltpu.make_async_copy(
        tok_hbm.at[:, pl.ds(pl.multiple_of(core * half, half), half)], tok, load_sem.at[0]
    )
    loads = []
    for part in range(2):
        for i, source in enumerate((w_hbm, q_hbm)):
            loads.append(
                pltpu.make_async_copy(
                    source.at[0, 0, pl.ds(part * half, half)],
                    wq.at[part, :, pl.ds(i * columns, columns)],
                    load_sem.at[1 + 2 * part + i],
                )
            )
    load_routes.start()
    load_tok.start()

    barrier = pltpu.get_barrier_semaphore()
    for k in range(1, SHIFTS):
        pl.semaphore_signal(barrier, 1, device_id=(shift(k), section, mp), device_id_type=MESH)
    for peer in (across, beside, twin):
        pl.semaphore_signal(barrier, 1, device_id=peer, device_id_type=MESH)

    expert = lax.broadcasted_iota(jnp.int32, (SHIFTS, token_total), 0)
    before = lax.broadcasted_iota(jnp.int32, (token_total, token_total), 0)
    after = lax.broadcasted_iota(jnp.int32, (token_total, token_total), 1)
    upper = jnp.where(before <= after, 1.0, 0.0).astype(jnp.bfloat16)
    mom[...] = jnp.zeros_like(mom)
    load_routes.wait()
    chosen = jnp.zeros((SHIFTS, token_total), jnp.float32)
    for i in range(routes.shape[0]):
        chosen += jnp.where(routes[i : i + 1, :] == expert, 1.0, 0.0)
    rank = jnp.dot(chosen.astype(jnp.bfloat16), upper, preferred_element_type=jnp.float32)
    places[...] = jnp.where(chosen > 0, rank - 1.0, -1.0)
    tally[...] = jnp.broadcast_to(jnp.sum(chosen, axis=1, keepdims=True), tally.shape)
    load_tok.wait()

    slot = lax.broadcasted_iota(jnp.int32, (PIECE, token_total), 0)

    def collect(group):
        start = jnp.where(group < SIDE, mine, PIECE - mine)
        number = (slot + start).astype(jnp.float32)
        picks = []
        for j in range(SIDE):
            line = places[pl.ds(shift(group * SIDE + j), 1), :]
            picks.append(jnp.where(line == number, 1.0, 0.0).astype(jnp.bfloat16))
        pick = jnp.concatenate(picks, axis=0)
        outbox[span(group, GROUP), :] = jnp.dot(
            pick, tok[...], preferred_element_type=jnp.float32
        ).astype(jnp.bfloat16)

    def launch(p, ready):
        @pl.when(ready & (p % SHIFTS > 0) & (p < 2 * SHIFTS))
        def _():
            a_copy(p).start()

    def own_piece(p):
        rows[core, span(p, PIECE), :] = outbox[span(p, PIECE), :]

    def carry(p):
        for i in range(2):
            x_copy(2 * p + i).start()

    for load in loads:
        load.start()
    collect(0)
    pl.semaphore_wait(barrier, SHIFTS + 2)
    for p in range(1, SIDE):
        a_copy(p).start()
    own_piece(0)
    carry(0)
    c_copy(0, core).start()

    @pl.loop(1, AHEAD // SIDE)
    def _(group):
        collect(group)
        for j in range(SIDE):
            launch(group * SIDE + j, True)

    collect(AHEAD // SIDE)
    for k in range(1, SHIFTS):
        t_copy(k).start()

    def part(group, i):
        return jnp.dot(rows[i, span(group, GROUP), :], wq[i], preferred_element_type=jnp.float32)

    def fold(values):
        return jnp.sum(values.reshape(GROUP // 8, 8, columns), axis=0)

    def begin(group):
        for j in range(SIDE):
            c_copy(group * SIDE + j, 1 - core).wait_recv()
        acc[...] = part(group, 0)

    def finish(group):
        acc[...] += part(group, 1)
        full = acc[:, :columns]
        quant = acc[:, columns:]
        mom[0] += fold(quant * quant)
        mom[1] += fold(quant)
        mom[2] += fold(quant * full)
        mom[3] += fold(full)

    def sent(k):
        for p in (2 * k, 2 * k + 1):

            @pl.when(p % SHIFTS > 0)
            def _():
                a_copy(p).wait_send()

            x_copy(p).wait_send()
            f_copy(p).wait_send()
        c_copy(k, core).wait_send()
        c_copy(2 * SHIFTS + k, core).wait_send()
        c_copy(3 * SHIFTS + k, core).wait_send()

    def arrive(p):
        a_copy(p).wait_recv()
        carry(p)
        c_copy(p, core).start()

    for p in range(1, EARLY + 1):
        arrive(p)

    def product(step, i):
        group = -1
        for at, groups in PRODUCTS.items():
            if len(groups) > i:
                group = jnp.where(step == at, groups[i], group)
        return group

    @pl.loop(0, STEPS)
    def _(step):
        first, second = product(step, 0), product(step, 1)

        def relay(u):
            @pl.when((step >= RELAY_LAG) & (step < SHIFTS + RELAY_LAG))
            def _():
                x_copy(u).wait_recv()
                f_copy(u).start()

        relay(2 * (step - RELAY_LAG))
        for j in range(2):
            launch(AHEAD + 2 * step + j, True)

        @pl.when(step == min(PRODUCTS))
        def _():
            for load in loads:
                load.wait()

        pl.when(first >= 0)(functools.partial(begin, first))

        @pl.when((step > 0) & (step + EARLY < SHIFTS))
        def _():
            arrive(step + EARLY)

        relay(2 * (step - RELAY_LAG) + 1)

        @pl.when((step >= RELAY_LAG) & (step < SHIFTS + RELAY_LAG))
        def _():
            c_copy(2 * SHIFTS + step - RELAY_LAG, core).start()

        @pl.when((step >= HAND_LAG) & (step < SHIFTS + HAND_LAG))
        def _():
            k = step - HAND_LAG
            for i in range(2):
                f_copy(2 * k + i).wait_recv()
            c_copy(3 * SHIFTS + k, core).start()

        @pl.when((step % 2 == 1) & (step < STEPS_SEND - 2))
        def _():
            group = AHEAD // SIDE + (step + 1) // 2
            collect(group)

            @pl.when(group == SIDE)
            def _():
                own_piece(SHIFTS)
                c_copy(SHIFTS, core).start()

        pl.when(first >= 0)(functools.partial(finish, first))

        @pl.when(second >= 0)
        def _():
            begin(second)
            finish(second)

        @pl.when((step >= REST) & (step < REST + SHIFTS // 2))
        def _():
            for j in range(2):
                p = SHIFTS + 2 * (step - REST) + j

                @pl.when(p > SHIFTS)
                def _():
                    a_copy(p).wait_recv()
                    c_copy(p, core).start()

        @pl.when((step >= SENT_LAG) & (step < SHIFTS))
        def _():
            sent(step - SENT_LAG)

        @pl.when(step == SHIFTS // 2)
        def _():
            total = tally[...]
            for k in range(1, SHIFTS):
                t_copy(k).wait()
                total += tally_in[k]
            tally_in[0] = total
            u_copy().start()

    u_copy().wait()
    total = tally_in[0] + tally_other[...]
    named = lax.broadcasted_iota(jnp.int32, total.shape, 0)
    counts = jnp.sum(jnp.where(named == dp, total, 0.0), axis=0, keepdims=True)[:, :1]
    for i in range(4):
        out_ref[i : i + 1, :] = jnp.sum(mom[i], axis=0, keepdims=True)
    out_ref[4:, :] = jnp.broadcast_to(counts, (4, columns))

    for k in range(SHIFTS - SENT_LAG, SHIFTS):
        sent(k)
    for k in range(SHIFTS):
        c_copy(SHIFTS + k, core).wait_send()


def refit_columns(sums):
    square, first_moment, cross_term, target, counts = (sums[i] for i in range(5))
    denominator = counts + RIDGE
    diagonal = square + RIDGE
    anchored = cross_term + RIDGE
    determinant = diagonal * denominator - first_moment * first_moment
    refit_scale = (denominator * anchored - first_moment * target) / determinant
    refit_bias = (diagonal * target - first_moment * anchored) / determinant
    return refit_scale[None, None], refit_bias[None, None]


def local(tokens, routes, weight, quantized):
    token_total, width = tokens.shape
    columns = weight.shape[-1]
    vmem = pl.BlockSpec(memory_space=pltpu.VMEM)
    hbm = pl.BlockSpec(memory_space=pl.ANY)
    sems = pltpu.SemaphoreType.DMA
    sums = pl.pallas_call(
        kernel,
        out_shape=jax.ShapeDtypeStruct((8, columns), jnp.float32),
        in_specs=[hbm, hbm, hbm, hbm],
        out_specs=vmem,
        scratch_shapes=[
            pltpu.VMEM(routes.T.shape, jnp.int32),
            pltpu.VMEM((token_total, width // 2), jnp.bfloat16),
            pltpu.VMEM((2, width // 2, 2 * columns), jnp.bfloat16),
            pltpu.VMEM((SHIFTS * CAP, width // 2), jnp.bfloat16),
            pltpu.VMEM((2, 2 * SHIFTS * CAP, width // 2), jnp.bfloat16),
            pltpu.VMEM((SHIFTS, token_total), jnp.float32),
            pltpu.VMEM((GROUP, 2 * columns), jnp.float32),
            pltpu.VMEM((4, 8, columns), jnp.float32),
            pltpu.VMEM((SHIFTS, 128), jnp.float32),
            pltpu.VMEM((SHIFTS, SHIFTS, 128), jnp.float32),
            pltpu.VMEM((SHIFTS, 128), jnp.float32),
            sems((6,)),
        ]
        + [sems((2 * SHIFTS,))] * 6
        + [sems((4 * SHIFTS,))] * 2
        + [sems((SHIFTS,))] * 2
        + [sems((2,))],
        compiler_params=pltpu.CompilerParams(
            collective_id=0, has_side_effects=True, vmem_limit_bytes=56 << 20
        ),
        cost_estimate=pl.CostEstimate(
            flops=2 * 2048 * 4096 * 768, bytes_accessed=10 << 20, transcendentals=0
        ),
    )(tokens, routes.T, weight, quantized)
    return refit_columns(sums)


def solution(mesh):
    placed = (
        P(("dp", "section"), None),
        P(("dp", "section"), None),
        P("section", "dp", None, "mp"),
        P("section", "dp", None, "mp"),
    )
    return jax.shard_map(
        local,
        mesh=mesh,
        in_specs=placed,
        out_specs=(P("section", "dp", "mp"), P("section", "dp", "mp")),
        check_vma=False,
    )
```

```python
import functools

import jax
import jax.numpy as jnp
from jax import lax
from jax.experimental import pallas as pl
from jax.experimental.pallas import tpu as pltpu
from jax.sharding import PartitionSpec as P

CAP = 64
RIDGE = 1.0
MESH = pl.DeviceIdType.MESH
SIDE = 4
SHIFTS = SIDE * SIDE
PIECE = CAP // 2
UNIT = PIECE // 2
GROUP = SIDE * PIECE
PRODUCTS = {
    2: (0,), 5: (8,), 6: (1,), 8: (12,), 9: (9,), 10: (2,), 11: (13,), 13: (10, 4),
    14: (3,), 15: (5,), 16: (14,), 17: (6, 11), 19: (7, 15),
}
STEPS = 20
NEAREST = (
    (0, 0), (1, 0), (0, 1), (3, 0), (0, 3), (1, 1), (3, 3), (1, 3),
    (3, 1), (2, 0), (0, 2), (1, 2), (2, 1), (3, 2), (2, 3), (2, 2),
)
SHIFT_ORDER = NEAREST + NEAREST
EARLY = 2
REST = 11
AHEAD = 8
STEPS_SEND = (2 * SHIFTS - AHEAD) // 2
RELAY_LAG = 1
HAND_LAG = 3


def kernel(
    tok_hbm,
    routes_hbm,
    w_hbm,
    q_hbm,
    out_ref,
    routes,
    tok,
    wq,
    outbox,
    rows,
    places,
    acc,
    mom,
    tally,
    tally_in,
    tally_other,
    load_sem,
    a_send,
    a_recv,
    x_send,
    x_recv,
    f_send,
    f_recv,
    c_send,
    c_recv,
    t_sem,
    u_sem,
):
    dp, section, mp = lax.axis_index("dp"), lax.axis_index("section"), lax.axis_index("mp")
    y, z = dp // SIDE, dp % SIDE
    x_lo, core = mp // 2, mp % 2
    half = tok.shape[1]
    token_total = tok.shape[0]
    columns = w_hbm.shape[-1]

    across = (dp, 1 - section, (1 - x_lo) * 2 + core)
    beside = (dp, section, (1 - x_lo) * 2 + core)
    twin = (dp, section, x_lo * 2 + 1 - core)
    mine = jnp.where(section == x_lo, 0, PIECE)

    def shift(k):
        if isinstance(k, int):
            code = SHIFT_ORDER[k][0] * SIDE + SHIFT_ORDER[k][1]
        else:
            code = 0
            for i, (dy, dz) in enumerate(SHIFT_ORDER):
                code = jnp.where(k == i, dy * SIDE + dz, code)
        return ((y + code // SIDE) % SIDE) * SIDE + (z + code % SIDE) % SIDE

    def span(index, size):
        return pl.ds(pl.multiple_of(index * size, size), size)

    def remote(source, target, send, recv, device):
        return pltpu.make_async_remote_copy(source, target, send, recv, device, MESH)

    def a_copy(p):
        return remote(
            outbox.at[span(p, PIECE)],
            rows.at[core, span(p, PIECE)],
            a_send.at[0],
            a_recv.at[jnp.where(p < SHIFTS, p, SHIFTS + (p - SHIFTS) // 2)],
            (shift(p), section, mp),
        )

    def t_copy(k):
        return remote(tally, tally_in.at[k], t_sem.at[0], t_sem.at[1], (shift(k), section, mp))

    def u_copy():
        return remote(tally_in.at[0], tally_other, u_sem.at[0], u_sem.at[1], across)

    units = SHIFTS * PIECE // UNIT

    def x_copy(u):
        return remote(
            rows.at[core, span(u, UNIT)],
            rows.at[core, span(2 * units + u, UNIT)],
            x_send.at[0],
            x_recv.at[u],
            across,
        )

    def f_copy(u):
        return remote(
            rows.at[core, span(2 * units + u, UNIT)],
            rows.at[core, span(3 * units + u, UNIT)],
            f_send.at[0],
            f_recv.at[u // 2],
            beside,
        )

    def c_copy(p, size=PIECE):
        place = pl.ds(pl.multiple_of(p * PIECE, PIECE), size)
        return remote(
            rows.at[core, place],
            rows.at[core, place],
            c_send.at[0],
            c_recv.at[p // SIDE],
            twin,
        )

    def await_bytes(ref, sem):
        pltpu.make_async_copy(ref, ref, sem).wait()

    load_routes = pltpu.make_async_copy(routes_hbm, routes, load_sem.at[2])
    load_tok = pltpu.make_async_copy(
        tok_hbm.at[:, pl.ds(pl.multiple_of(core * half, half), half)], tok, load_sem.at[0]
    )
    loads = []
    for part in range(2):
        for i, source in enumerate((w_hbm, q_hbm)):
            loads.append(
                pltpu.make_async_copy(
                    source.at[0, 0, pl.ds(part * half, half)],
                    wq.at[part, :, pl.ds(i * columns, columns)],
                    load_sem.at[1],
                )
            )
    load_routes.start()
    load_tok.start()

    barrier = pltpu.get_barrier_semaphore()
    for k in range(1, SHIFTS):
        pl.semaphore_signal(barrier, 1, device_id=(shift(k), section, mp), device_id_type=MESH)
    for peer in (across, beside, twin):
        pl.semaphore_signal(barrier, 1, device_id=peer, device_id_type=MESH)

    expert = lax.broadcasted_iota(jnp.int32, (SHIFTS, token_total), 0)
    before = lax.broadcasted_iota(jnp.int32, (token_total, token_total), 0)
    after = lax.broadcasted_iota(jnp.int32, (token_total, token_total), 1)
    upper = jnp.where(before <= after, 1.0, 0.0).astype(jnp.bfloat16)
    mom[...] = jnp.zeros_like(mom)
    load_routes.wait()
    chosen = jnp.zeros((SHIFTS, token_total), jnp.float32)
    for i in range(routes.shape[0]):
        chosen += jnp.where(routes[i : i + 1, :] == expert, 1.0, 0.0)
    rank = jnp.dot(chosen.astype(jnp.bfloat16), upper, preferred_element_type=jnp.float32)
    places[...] = jnp.where(chosen > 0, rank - 1.0, -1.0)
    tally[...] = jnp.broadcast_to(jnp.sum(chosen, axis=1, keepdims=True), tally.shape)
    load_tok.wait()

    slot = lax.broadcasted_iota(jnp.int32, (PIECE, token_total), 0)

    def collect(group):
        start = jnp.where(group < SIDE, mine, PIECE - mine)
        number = (slot + start).astype(jnp.float32)
        picks = []
        for j in range(SIDE):
            line = places[pl.ds(shift(group * SIDE + j), 1), :]
            picks.append(jnp.where(line == number, 1.0, 0.0).astype(jnp.bfloat16))
        pick = jnp.concatenate(picks, axis=0)
        outbox[span(group, GROUP), :] = jnp.dot(
            pick, tok[...], preferred_element_type=jnp.float32
        ).astype(jnp.bfloat16)

    def launch(p, ready):
        @pl.when(ready & (p % SHIFTS > 0) & (p < 2 * SHIFTS))
        def _():
            a_copy(p).start()

    def own_piece(p):
        rows[core, span(p, PIECE), :] = outbox[span(p, PIECE), :]

    def carry(p):
        for i in range(2):
            x_copy(2 * p + i).start()

    for load in loads:
        load.start()
    collect(0)
    pl.semaphore_wait(barrier, SHIFTS + 2)
    for p in range(1, SIDE):
        a_copy(p).start()
    own_piece(0)
    carry(0)
    c_copy(0).start()

    @pl.loop(1, AHEAD // SIDE)
    def _(group):
        collect(group)
        for j in range(SIDE):
            launch(group * SIDE + j, True)

    collect(AHEAD // SIDE)
    for k in range(1, SHIFTS):
        t_copy(k).start()

    def part(group, i):
        return jnp.dot(rows[i, span(group, GROUP), :], wq[i], preferred_element_type=jnp.float32)

    def fold(values):
        return jnp.sum(values.reshape(GROUP // 8, 8, columns), axis=0)

    def begin(group):
        await_bytes(rows.at[1 - core, span(group, GROUP)], c_recv.at[group])
        acc[...] = part(group, 0)

    def finish(group):
        acc[...] += part(group, 1)
        full = acc[:, :columns]
        quant = acc[:, columns:]
        mom[0] += fold(quant * quant)
        mom[1] += fold(quant)
        mom[2] += fold(quant * full)
        mom[3] += fold(full)

    def arrive(p):
        a_copy(p).wait_recv()
        carry(p)
        c_copy(p).start()

    for p in range(1, EARLY + 1):
        arrive(p)

    def product(step, i):
        group = -1
        for at, groups in PRODUCTS.items():
            if len(groups) > i:
                group = jnp.where(step == at, groups[i], group)
        return group

    @pl.loop(0, STEPS)
    def _(step):
        first, second = product(step, 0), product(step, 1)

        def relay(u):
            @pl.when((step >= RELAY_LAG) & (step < SHIFTS + RELAY_LAG))
            def _():
                x_copy(u).wait_recv()
                f_copy(u).start()

        relay(2 * (step - RELAY_LAG))
        for j in range(2):
            launch(AHEAD + 2 * step + j, True)

        @pl.when(step == min(PRODUCTS))
        def _():
            await_bytes(wq, load_sem.at[1])

        pl.when(first >= 0)(functools.partial(begin, first))

        @pl.when((step > 0) & (step + EARLY < SHIFTS))
        def _():
            arrive(step + EARLY)

        relay(2 * (step - RELAY_LAG) + 1)

        @pl.when((step >= RELAY_LAG) & (step < SHIFTS + RELAY_LAG))
        def _():
            c_copy(2 * SHIFTS + step - RELAY_LAG).start()

        @pl.when((step >= HAND_LAG) & (step < SHIFTS + HAND_LAG))
        def _():
            k = step - HAND_LAG
            await_bytes(rows.at[core, span(3 * SHIFTS + k, PIECE)], f_recv.at[k])
            c_copy(3 * SHIFTS + k).start()

        @pl.when((step % 2 == 1) & (step < STEPS_SEND - 2))
        def _():
            group = AHEAD // SIDE + (step + 1) // 2
            collect(group)

            @pl.when(group == SIDE)
            def _():
                own_piece(SHIFTS)
                c_copy(SHIFTS).start()

        pl.when(first >= 0)(functools.partial(finish, first))

        @pl.when(second >= 0)
        def _():
            begin(second)
            finish(second)

        @pl.when(step == REST)
        def _():
            a_copy(SHIFTS + 1).wait_recv()
            c_copy(SHIFTS + 1).start()

        @pl.when((step > REST) & (step < REST + SHIFTS // 2))
        def _():
            p = SHIFTS + 2 * (step - REST)
            await_bytes(
                rows.at[core, pl.ds(pl.multiple_of(p * PIECE, PIECE), 2 * PIECE)],
                a_recv.at[SHIFTS + step - REST],
            )
            c_copy(p, 2 * PIECE).start()

        @pl.when(step == SHIFTS // 2)
        def _():
            await_bytes(tally_in.at[pl.ds(1, SHIFTS - 1)], t_sem.at[1])
            total = tally[...]
            for k in range(1, SHIFTS):
                total += tally_in[k]
            tally_in[0] = total
            u_copy().start()

    u_copy().wait()
    total = tally_in[0] + tally_other[...]
    named = lax.broadcasted_iota(jnp.int32, total.shape, 0)
    counts = jnp.sum(jnp.where(named == dp, total, 0.0), axis=0, keepdims=True)[:, :1]
    for i in range(4):
        out_ref[i : i + 1, :] = jnp.sum(mom[i], axis=0, keepdims=True)
    out_ref[4:, :] = jnp.broadcast_to(counts, (4, columns))

    await_bytes(outbox.at[pl.ds(0, (SHIFTS - 1) * CAP)], a_send.at[0])
    await_bytes(tally_in.at[pl.ds(1, SHIFTS - 1)], t_sem.at[0])
    await_bytes(rows.at[0, pl.ds(0, SHIFTS * PIECE)], x_send.at[0])
    await_bytes(rows.at[0, pl.ds(0, SHIFTS * PIECE)], f_send.at[0])
    await_bytes(rows.at[0], c_send.at[0])


def refit_columns(sums):
    square, first_moment, cross_term, target, counts = (sums[i] for i in range(5))
    denominator = counts + RIDGE
    diagonal = square + RIDGE
    anchored = cross_term + RIDGE
    determinant = diagonal * denominator - first_moment * first_moment
    refit_scale = (denominator * anchored - first_moment * target) / determinant
    refit_bias = (diagonal * target - first_moment * anchored) / determinant
    return refit_scale[None, None], refit_bias[None, None]


def local(tokens, routes, weight, quantized):
    token_total, width = tokens.shape
    columns = weight.shape[-1]
    vmem = pl.BlockSpec(memory_space=pltpu.VMEM)
    hbm = pl.BlockSpec(memory_space=pl.ANY)
    sems = pltpu.SemaphoreType.DMA
    sums = pl.pallas_call(
        kernel,
        out_shape=jax.ShapeDtypeStruct((8, columns), jnp.float32),
        in_specs=[hbm, hbm, hbm, hbm],
        out_specs=vmem,
        scratch_shapes=[
            pltpu.VMEM(routes.T.shape, jnp.int32),
            pltpu.VMEM((token_total, width // 2), jnp.bfloat16),
            pltpu.VMEM((2, width // 2, 2 * columns), jnp.bfloat16),
            pltpu.VMEM((SHIFTS * CAP, width // 2), jnp.bfloat16),
            pltpu.VMEM((2, 2 * SHIFTS * CAP, width // 2), jnp.bfloat16),
            pltpu.VMEM((SHIFTS, token_total), jnp.float32),
            pltpu.VMEM((GROUP, 2 * columns), jnp.float32),
            pltpu.VMEM((4, 8, columns), jnp.float32),
            pltpu.VMEM((SHIFTS, 128), jnp.float32),
            pltpu.VMEM((SHIFTS, SHIFTS, 128), jnp.float32),
            pltpu.VMEM((SHIFTS, 128), jnp.float32),
            sems((3,)),
            sems((1,)),
            sems((SHIFTS + SHIFTS // 2,)),
            sems((1,)),
            sems((2 * SHIFTS,)),
            sems((1,)),
            sems((SHIFTS,)),
            sems((1,)),
            sems((SHIFTS,)),
            sems((2,)),
            sems((2,)),
        ],
        compiler_params=pltpu.CompilerParams(
            collective_id=0, has_side_effects=True, vmem_limit_bytes=56 << 20
        ),
        cost_estimate=pl.CostEstimate(
            flops=2 * 2048 * 4096 * 768, bytes_accessed=10 << 20, transcendentals=0
        ),
    )(tokens, routes.T, weight, quantized)
    return refit_columns(sums)


def solution(mesh):
    placed = (
        P(("dp", "section"), None),
        P(("dp", "section"), None),
        P("section", "dp", None, "mp"),
        P("section", "dp", None, "mp"),
    )
    return jax.shard_map(
        local,
        mesh=mesh,
        in_specs=placed,
        out_specs=(P("section", "dp", "mp"), P("section", "dp", "mp")),
        check_vma=False,
    )
```

```python
import functools

import jax
import jax.numpy as jnp
from jax import lax
from jax.experimental import pallas as pl
from jax.experimental.pallas import tpu as pltpu
from jax.sharding import PartitionSpec as P

CAP = 64
RIDGE = 1.0
MESH = pl.DeviceIdType.MESH
SIDE = 4
SHIFTS = SIDE * SIDE
PIECE = CAP // 2
UNIT = PIECE // 2
GROUP = SIDE * PIECE
PRODUCTS = {
    2: (0,), 5: (8,), 6: (1,), 8: (12,), 9: (9,), 10: (2,), 11: (13,), 13: (10, 4),
    14: (3,), 15: (5,), 16: (14,), 17: (6, 11), 19: (7, 15),
}
STEPS = 20
NEAREST = (
    (0, 0), (1, 0), (0, 1), (3, 0), (0, 3), (1, 1), (3, 3), (1, 3),
    (3, 1), (2, 0), (0, 2), (1, 2), (2, 1), (3, 2), (2, 3), (2, 2),
)
SHIFT_ORDER = NEAREST + NEAREST
EARLY = 2
REST = 11
AHEAD = 8
STEPS_SEND = (2 * SHIFTS - AHEAD) // 2
RELAY_LAG = 1
HAND_LAG = 3


def kernel(
    tok_hbm,
    routes_hbm,
    w_hbm,
    q_hbm,
    out_ref,
    routes,
    tok,
    wq,
    outbox,
    rows,
    places,
    acc,
    mom,
    tally,
    tally_in,
    tally_other,
    load_sem,
    a_send,
    a_recv,
    x_send,
    x_recv,
    f_send,
    f_recv,
    c_send,
    c_recv,
    t_sem,
    u_sem,
):
    dp, section, mp = lax.axis_index("dp"), lax.axis_index("section"), lax.axis_index("mp")
    y, z = dp // SIDE, dp % SIDE
    x_lo, core = mp // 2, mp % 2
    half = tok.shape[1]
    token_total = tok.shape[0]
    columns = w_hbm.shape[-1]

    across = (dp, 1 - section, (1 - x_lo) * 2 + core)
    beside = (dp, section, (1 - x_lo) * 2 + core)
    twin = (dp, section, x_lo * 2 + 1 - core)
    mine = jnp.where(section == x_lo, 0, PIECE)

    def shift(k):
        if isinstance(k, int):
            code = SHIFT_ORDER[k][0] * SIDE + SHIFT_ORDER[k][1]
        else:
            code = 0
            for i, (dy, dz) in enumerate(SHIFT_ORDER):
                code = jnp.where(k == i, dy * SIDE + dz, code)
        return ((y + code // SIDE) % SIDE) * SIDE + (z + code % SIDE) % SIDE

    def span(index, size):
        return pl.ds(pl.multiple_of(index * size, size), size)

    def remote(source, target, send, recv, device):
        return pltpu.make_async_remote_copy(source, target, send, recv, device, MESH)

    def a_copy(p):
        return remote(
            outbox.at[span(p, PIECE)],
            rows.at[core, span(p, PIECE)],
            a_send.at[0],
            a_recv.at[jnp.where(p < SHIFTS, p, SHIFTS + (p - SHIFTS) // 2)],
            (shift(p), section, mp),
        )

    def t_copy(k):
        return remote(tally, tally_in.at[k], t_sem.at[0], t_sem.at[1], (shift(k), section, mp))

    def u_copy():
        return remote(tally_in.at[0], tally_other, u_sem.at[0], u_sem.at[1], across)

    units = SHIFTS * PIECE // UNIT

    def x_copy(u):
        return remote(
            rows.at[core, span(u, UNIT)],
            rows.at[core, span(2 * units + u, UNIT)],
            x_send.at[0],
            x_recv.at[u],
            across,
        )

    def f_copy(u):
        return remote(
            rows.at[core, span(2 * units + u, UNIT)],
            rows.at[core, span(3 * units + u, UNIT)],
            f_send.at[0],
            f_recv.at[u // 2],
            beside,
        )

    def c_copy(p, size=PIECE):
        place = pl.ds(pl.multiple_of(p * PIECE, PIECE), size)
        return remote(
            rows.at[core, place],
            rows.at[core, place],
            c_send.at[0],
            c_recv.at[p // SIDE],
            twin,
        )

    def await_bytes(ref, sem):
        pltpu.make_async_copy(ref, ref, sem).wait()

    load_routes = pltpu.make_async_copy(routes_hbm, routes, load_sem.at[2])
    load_tok = pltpu.make_async_copy(
        tok_hbm.at[:, pl.ds(pl.multiple_of(core * half, half), half)], tok, load_sem.at[0]
    )
    loads = []
    for part in range(2):
        for i, source in enumerate((w_hbm, q_hbm)):
            loads.append(
                pltpu.make_async_copy(
                    source.at[0, 0, pl.ds(part * half, half)],
                    wq.at[part, :, pl.ds(i * columns, columns)],
                    load_sem.at[1],
                )
            )
    load_routes.start()
    load_tok.start()

    barrier = pltpu.get_barrier_semaphore()
    for k in range(1, SHIFTS):
        pl.semaphore_signal(barrier, 1, device_id=(shift(k), section, mp), device_id_type=MESH)
    for peer in (across, beside, twin):
        pl.semaphore_signal(barrier, 1, device_id=peer, device_id_type=MESH)

    expert = lax.broadcasted_iota(jnp.int32, (SHIFTS, token_total), 0)
    before = lax.broadcasted_iota(jnp.int32, (token_total, token_total), 0)
    after = lax.broadcasted_iota(jnp.int32, (token_total, token_total), 1)
    upper = jnp.where(before <= after, 1.0, 0.0).astype(jnp.bfloat16)
    mom[...] = jnp.zeros_like(mom)
    load_routes.wait()
    chosen = jnp.zeros((SHIFTS, token_total), jnp.float32)
    for i in range(routes.shape[0]):
        chosen += jnp.where(routes[i : i + 1, :] == expert, 1.0, 0.0)
    rank = jnp.dot(chosen.astype(jnp.bfloat16), upper, preferred_element_type=jnp.float32)
    places[...] = jnp.where(chosen > 0, rank - 1.0, -1.0)
    tally[...] = jnp.broadcast_to(jnp.sum(chosen, axis=1, keepdims=True), tally.shape)
    load_tok.wait()

    slot = lax.broadcasted_iota(jnp.int32, (PIECE, token_total), 0)

    def collect(group):
        start = jnp.where(group < SIDE, mine, PIECE - mine)
        number = (slot + start).astype(jnp.float32)
        picks = []
        for j in range(SIDE):
            line = places[pl.ds(shift(group * SIDE + j), 1), :]
            picks.append(jnp.where(line == number, 1.0, 0.0).astype(jnp.bfloat16))
        pick = jnp.concatenate(picks, axis=0)
        outbox[span(group, GROUP), :] = jnp.dot(
            pick, tok[...], preferred_element_type=jnp.float32
        ).astype(jnp.bfloat16)

    def launch(p, ready):
        @pl.when(ready & (p % SHIFTS > 0) & (p < 2 * SHIFTS))
        def _():
            a_copy(p).start()

    def own_piece(p):
        rows[core, span(p, PIECE), :] = outbox[span(p, PIECE), :]

    def carry(p):
        for i in range(2):
            x_copy(2 * p + i).start()

    for load in loads:
        load.start()
    collect(0)
    pl.semaphore_wait(barrier, SHIFTS + 2)
    for p in range(1, SIDE):
        a_copy(p).start()
    own_piece(0)
    carry(0)
    c_copy(0).start()

    @pl.loop(1, AHEAD // SIDE)
    def _(group):
        collect(group)
        for j in range(SIDE):
            launch(group * SIDE + j, True)

    collect(AHEAD // SIDE)
    for k in range(1, SHIFTS):
        t_copy(k).start()

    def part(group, i):
        return jnp.dot(rows[i, span(group, GROUP), :], wq[i], preferred_element_type=jnp.float32)

    def fold(values):
        return jnp.sum(values.reshape(GROUP // 8, 8, columns), axis=0)

    def begin(group):
        await_bytes(rows.at[1 - core, span(group, GROUP)], c_recv.at[group])
        acc[...] = part(group, 0)

    def finish(group):
        acc[...] += part(group, 1)
        full = acc[:, :columns]
        quant = acc[:, columns:]
        mom[0] += fold(quant * quant)
        mom[1] += fold(quant)
        mom[2] += fold(quant * full)
        mom[3] += fold(full)

    def arrive(p):
        a_copy(p).wait_recv()
        carry(p)
        c_copy(p).start()

    for p in range(1, EARLY + 1):
        arrive(p)

    def product(step, i):
        group = -1
        for at, groups in PRODUCTS.items():
            if len(groups) > i:
                group = jnp.where(step == at, groups[i], group)
        return group

    @pl.loop(0, STEPS)
    def _(step):
        first, second = product(step, 0), product(step, 1)

        def relay(u):
            @pl.when((step >= RELAY_LAG) & (step < SHIFTS + RELAY_LAG))
            def _():
                x_copy(u).wait_recv()
                f_copy(u).start()

        relay(2 * (step - RELAY_LAG))
        for j in range(2):
            launch(AHEAD + 2 * step + j, True)

        @pl.when(step == min(PRODUCTS))
        def _():
            await_bytes(wq, load_sem.at[1])

        @pl.when(step == REST)
        def _():
            a_copy(SHIFTS + 1).wait_recv()
            c_copy(SHIFTS + 1).start()

        @pl.when((step > REST) & (step < REST + SHIFTS // 2))
        def _():
            p = SHIFTS + 2 * (step - REST)
            await_bytes(
                rows.at[core, pl.ds(pl.multiple_of(p * PIECE, PIECE), 2 * PIECE)],
                a_recv.at[SHIFTS + step - REST],
            )
            c_copy(p, 2 * PIECE).start()

        pl.when(first >= 0)(functools.partial(begin, first))

        @pl.when((step > 0) & (step + EARLY < SHIFTS))
        def _():
            arrive(step + EARLY)

        relay(2 * (step - RELAY_LAG) + 1)

        @pl.when((step >= RELAY_LAG) & (step < SHIFTS + RELAY_LAG))
        def _():
            c_copy(2 * SHIFTS + step - RELAY_LAG).start()

        @pl.when((step >= HAND_LAG) & (step < SHIFTS + HAND_LAG))
        def _():
            k = step - HAND_LAG
            await_bytes(rows.at[core, span(3 * SHIFTS + k, PIECE)], f_recv.at[k])
            c_copy(3 * SHIFTS + k).start()

        @pl.when((step % 2 == 1) & (step < STEPS_SEND - 2))
        def _():
            group = AHEAD // SIDE + (step + 1) // 2
            collect(group)

            @pl.when(group == SIDE)
            def _():
                own_piece(SHIFTS)
                c_copy(SHIFTS).start()

        pl.when(first >= 0)(functools.partial(finish, first))

        @pl.when(second >= 0)
        def _():
            begin(second)
            finish(second)

        @pl.when(step == SHIFTS // 2)
        def _():
            await_bytes(tally_in.at[pl.ds(1, SHIFTS - 1)], t_sem.at[1])
            total = tally[...]
            for k in range(1, SHIFTS):
                total += tally_in[k]
            tally_in[0] = total
            u_copy().start()

    u_copy().wait()
    total = tally_in[0] + tally_other[...]
    named = lax.broadcasted_iota(jnp.int32, total.shape, 0)
    counts = jnp.sum(jnp.where(named == dp, total, 0.0), axis=0, keepdims=True)[:, :1]
    for i in range(4):
        out_ref[i : i + 1, :] = jnp.sum(mom[i], axis=0, keepdims=True)
    out_ref[4:, :] = jnp.broadcast_to(counts, (4, columns))

    await_bytes(outbox.at[pl.ds(0, (SHIFTS - 1) * CAP)], a_send.at[0])
    await_bytes(tally_in.at[pl.ds(1, SHIFTS - 1)], t_sem.at[0])
    await_bytes(rows.at[0, pl.ds(0, SHIFTS * PIECE)], x_send.at[0])
    await_bytes(rows.at[0, pl.ds(0, SHIFTS * PIECE)], f_send.at[0])
    await_bytes(rows.at[0], c_send.at[0])


def refit_columns(sums):
    square, first_moment, cross_term, target, counts = (sums[i] for i in range(5))
    denominator = counts + RIDGE
    diagonal = square + RIDGE
    anchored = cross_term + RIDGE
    determinant = diagonal * denominator - first_moment * first_moment
    refit_scale = (denominator * anchored - first_moment * target) / determinant
    refit_bias = (diagonal * target - first_moment * anchored) / determinant
    return refit_scale[None, None], refit_bias[None, None]


def local(tokens, routes, weight, quantized):
    token_total, width = tokens.shape
    columns = weight.shape[-1]
    vmem = pl.BlockSpec(memory_space=pltpu.VMEM)
    hbm = pl.BlockSpec(memory_space=pl.ANY)
    sems = pltpu.SemaphoreType.DMA
    sums = pl.pallas_call(
        kernel,
        out_shape=jax.ShapeDtypeStruct((8, columns), jnp.float32),
        in_specs=[hbm, hbm, hbm, hbm],
        out_specs=vmem,
        scratch_shapes=[
            pltpu.VMEM(routes.T.shape, jnp.int32),
            pltpu.VMEM((token_total, width // 2), jnp.bfloat16),
            pltpu.VMEM((2, width // 2, 2 * columns), jnp.bfloat16),
            pltpu.VMEM((SHIFTS * CAP, width // 2), jnp.bfloat16),
            pltpu.VMEM((2, 2 * SHIFTS * CAP, width // 2), jnp.bfloat16),
            pltpu.VMEM((SHIFTS, token_total), jnp.float32),
            pltpu.VMEM((GROUP, 2 * columns), jnp.float32),
            pltpu.VMEM((4, 8, columns), jnp.float32),
            pltpu.VMEM((SHIFTS, 128), jnp.float32),
            pltpu.VMEM((SHIFTS, SHIFTS, 128), jnp.float32),
            pltpu.VMEM((SHIFTS, 128), jnp.float32),
            sems((3,)),
            sems((1,)),
            sems((SHIFTS + SHIFTS // 2,)),
            sems((1,)),
            sems((2 * SHIFTS,)),
            sems((1,)),
            sems((SHIFTS,)),
            sems((1,)),
            sems((SHIFTS,)),
            sems((2,)),
            sems((2,)),
        ],
        compiler_params=pltpu.CompilerParams(
            collective_id=0, has_side_effects=True, vmem_limit_bytes=56 << 20
        ),
        cost_estimate=pl.CostEstimate(
            flops=2 * 2048 * 4096 * 768, bytes_accessed=10 << 20, transcendentals=0
        ),
    )(tokens, routes.T, weight, quantized)
    return refit_columns(sums)


def solution(mesh):
    placed = (
        P(("dp", "section"), None),
        P(("dp", "section"), None),
        P("section", "dp", None, "mp"),
        P("section", "dp", None, "mp"),
    )
    return jax.shard_map(
        local,
        mesh=mesh,
        in_specs=placed,
        out_specs=(P("section", "dp", "mp"), P("section", "dp", "mp")),
        check_vma=False,
    )
```

```python
import functools

import jax
import jax.numpy as jnp
from jax import lax
from jax.experimental import pallas as pl
from jax.experimental.pallas import tpu as pltpu
from jax.sharding import PartitionSpec as P

CAP = 64
RIDGE = 1.0
MESH = pl.DeviceIdType.MESH
SIDE = 4
SHIFTS = SIDE * SIDE
PIECE = CAP // 2
UNIT = PIECE // 2
GROUP = SIDE * PIECE
PRODUCTS = {
    2: (0,), 5: (8,), 6: (1,), 8: (12,), 9: (9,), 10: (2,), 11: (13,), 13: (10, 4),
    14: (3,), 15: (5,), 16: (14,), 17: (6, 11), 19: (7, 15),
}
STEPS = 20
NEAREST = (
    (0, 0), (1, 0), (0, 1), (3, 0), (0, 3), (1, 1), (3, 3), (1, 3),
    (3, 1), (2, 0), (0, 2), (1, 2), (2, 1), (3, 2), (2, 3), (2, 2),
)
SHIFT_ORDER = NEAREST + NEAREST
EARLY = 2
PARTS = 4
REST = 11
AHEAD = 8
STEPS_SEND = (2 * SHIFTS - AHEAD) // 2
RELAY_LAG = 1
HAND_LAG = 3


def kernel(
    tok_hbm,
    routes_hbm,
    w_hbm,
    q_hbm,
    out_ref,
    routes,
    tok,
    wq,
    outbox,
    rows,
    places,
    acc,
    mom,
    tally,
    tally_in,
    tally_other,
    load_sem,
    a_send,
    a_recv,
    x_send,
    x_recv,
    f_send,
    f_recv,
    c_send,
    c_recv,
    t_sem,
    u_sem,
):
    dp, section, mp = lax.axis_index("dp"), lax.axis_index("section"), lax.axis_index("mp")
    y, z = dp // SIDE, dp % SIDE
    x_lo, core = mp // 2, mp % 2
    half = tok.shape[1]
    token_total = tok.shape[0]
    columns = w_hbm.shape[-1]

    across = (dp, 1 - section, (1 - x_lo) * 2 + core)
    beside = (dp, section, (1 - x_lo) * 2 + core)
    twin = (dp, section, x_lo * 2 + 1 - core)
    mine = jnp.where(section == x_lo, 0, PIECE)

    def shift(k):
        if isinstance(k, int):
            code = SHIFT_ORDER[k][0] * SIDE + SHIFT_ORDER[k][1]
        else:
            code = 0
            for i, (dy, dz) in enumerate(SHIFT_ORDER):
                code = jnp.where(k == i, dy * SIDE + dz, code)
        return ((y + code // SIDE) % SIDE) * SIDE + (z + code % SIDE) % SIDE

    def span(index, size):
        return pl.ds(pl.multiple_of(index * size, size), size)

    def remote(source, target, send, recv, device):
        return pltpu.make_async_remote_copy(source, target, send, recv, device, MESH)

    def a_copy(p):
        return remote(
            outbox.at[span(p, PIECE)],
            rows.at[core, span(p, PIECE)],
            a_send.at[0],
            a_recv.at[jnp.where(p < SHIFTS, p, SHIFTS + (p - SHIFTS) // 2)],
            (shift(p), section, mp),
        )

    def t_copy(k):
        return remote(tally, tally_in.at[k], t_sem.at[0], t_sem.at[1], (shift(k), section, mp))

    def u_copy():
        return remote(tally_in.at[0], tally_other, u_sem.at[0], u_sem.at[1], across)

    units = SHIFTS * PIECE // UNIT

    def x_copy(u):
        return remote(
            rows.at[core, span(u, UNIT)],
            rows.at[core, span(2 * units + u, UNIT)],
            x_send.at[0],
            x_recv.at[u],
            across,
        )

    def f_copy(u):
        return remote(
            rows.at[core, span(2 * units + u, UNIT)],
            rows.at[core, span(3 * units + u, UNIT)],
            f_send.at[0],
            f_recv.at[u // 2],
            beside,
        )

    def c_copy(p, size=PIECE, parts=1):
        for i in range(parts):
            place = rows.at[
                core,
                pl.ds(pl.multiple_of(p * PIECE, PIECE), size),
                pl.ds(i * half // parts, half // parts),
            ]
            remote(place, place, c_send.at[0], c_recv.at[p // SIDE], twin).start()

    def await_bytes(ref, sem):
        pltpu.make_async_copy(ref, ref, sem).wait()

    load_routes = pltpu.make_async_copy(routes_hbm, routes, load_sem.at[2])
    load_tok = pltpu.make_async_copy(
        tok_hbm.at[:, pl.ds(pl.multiple_of(core * half, half), half)], tok, load_sem.at[0]
    )
    loads = []
    for part in range(2):
        for i, source in enumerate((w_hbm, q_hbm)):
            loads.append(
                pltpu.make_async_copy(
                    source.at[0, 0, pl.ds(part * half, half)],
                    wq.at[part, :, pl.ds(i * columns, columns)],
                    load_sem.at[1],
                )
            )
    load_routes.start()
    load_tok.start()

    barrier = pltpu.get_barrier_semaphore()
    for k in range(1, SHIFTS):
        pl.semaphore_signal(barrier, 1, device_id=(shift(k), section, mp), device_id_type=MESH)
    for peer in (across, beside, twin):
        pl.semaphore_signal(barrier, 1, device_id=peer, device_id_type=MESH)

    expert = lax.broadcasted_iota(jnp.int32, (SHIFTS, token_total), 0)
    before = lax.broadcasted_iota(jnp.int32, (token_total, token_total), 0)
    after = lax.broadcasted_iota(jnp.int32, (token_total, token_total), 1)
    upper = jnp.where(before <= after, 1.0, 0.0).astype(jnp.bfloat16)
    mom[...] = jnp.zeros_like(mom)
    load_routes.wait()
    chosen = jnp.zeros((SHIFTS, token_total), jnp.float32)
    for i in range(routes.shape[0]):
        chosen += jnp.where(routes[i : i + 1, :] == expert, 1.0, 0.0)
    rank = jnp.dot(chosen.astype(jnp.bfloat16), upper, preferred_element_type=jnp.float32)
    places[...] = jnp.where(chosen > 0, rank - 1.0, -1.0)
    tally[...] = jnp.broadcast_to(jnp.sum(chosen, axis=1, keepdims=True), tally.shape)
    load_tok.wait()

    slot = lax.broadcasted_iota(jnp.int32, (PIECE, token_total), 0)

    def collect(group):
        start = jnp.where(group < SIDE, mine, PIECE - mine)
        number = (slot + start).astype(jnp.float32)
        picks = []
        for j in range(SIDE):
            line = places[pl.ds(shift(group * SIDE + j), 1), :]
            picks.append(jnp.where(line == number, 1.0, 0.0).astype(jnp.bfloat16))
        pick = jnp.concatenate(picks, axis=0)
        outbox[span(group, GROUP), :] = jnp.dot(
            pick, tok[...], preferred_element_type=jnp.float32
        ).astype(jnp.bfloat16)

    def launch(p, ready):
        @pl.when(ready & (p % SHIFTS > 0) & (p < 2 * SHIFTS))
        def _():
            a_copy(p).start()

    def own_piece(p):
        rows[core, span(p, PIECE), :] = outbox[span(p, PIECE), :]

    def carry(p):
        for i in range(2):
            x_copy(2 * p + i).start()

    for load in loads:
        load.start()
    collect(0)
    pl.semaphore_wait(barrier, SHIFTS + 2)
    for p in range(1, SIDE):
        a_copy(p).start()
    own_piece(0)
    carry(0)
    c_copy(0)

    @pl.loop(1, AHEAD // SIDE)
    def _(group):
        collect(group)
        for j in range(SIDE):
            launch(group * SIDE + j, True)

    collect(AHEAD // SIDE)
    for k in range(1, SHIFTS):
        t_copy(k).start()

    def part(group, i):
        return jnp.dot(rows[i, span(group, GROUP), :], wq[i], preferred_element_type=jnp.float32)

    def fold(values):
        return jnp.sum(values.reshape(GROUP // 8, 8, columns), axis=0)

    def begin(group):
        await_bytes(rows.at[1 - core, span(group, GROUP)], c_recv.at[group])
        acc[...] = part(group, 0)

    def finish(group):
        acc[...] += part(group, 1)
        full = acc[:, :columns]
        quant = acc[:, columns:]
        mom[0] += fold(quant * quant)
        mom[1] += fold(quant)
        mom[2] += fold(quant * full)
        mom[3] += fold(full)

    def arrive(p):
        a_copy(p).wait_recv()
        carry(p)
        c_copy(p)

    for p in range(1, EARLY + 1):
        arrive(p)

    def product(step, i):
        group = -1
        for at, groups in PRODUCTS.items():
            if len(groups) > i:
                group = jnp.where(step == at, groups[i], group)
        return group

    @pl.loop(0, STEPS)
    def _(step):
        first, second = product(step, 0), product(step, 1)

        def relay(u):
            @pl.when((step >= RELAY_LAG) & (step < SHIFTS + RELAY_LAG))
            def _():
                x_copy(u).wait_recv()
                f_copy(u).start()

        relay(2 * (step - RELAY_LAG))
        for j in range(2):
            launch(AHEAD + 2 * step + j, True)

        @pl.when(step == min(PRODUCTS))
        def _():
            await_bytes(wq, load_sem.at[1])

        @pl.when(step == REST)
        def _():
            a_copy(SHIFTS + 1).wait_recv()
            c_copy(SHIFTS + 1)

        @pl.when((step > REST) & (step < REST + SHIFTS // 2))
        def _():
            p = SHIFTS + 2 * (step - REST)
            await_bytes(
                rows.at[core, pl.ds(pl.multiple_of(p * PIECE, PIECE), 2 * PIECE)],
                a_recv.at[SHIFTS + step - REST],
            )
            c_copy(p, 2 * PIECE, 2 * PARTS)

        pl.when(first >= 0)(functools.partial(begin, first))

        @pl.when((step > 0) & (step + EARLY < SHIFTS))
        def _():
            arrive(step + EARLY)

        relay(2 * (step - RELAY_LAG) + 1)

        @pl.when((step >= RELAY_LAG) & (step < SHIFTS + RELAY_LAG))
        def _():
            c_copy(2 * SHIFTS + step - RELAY_LAG, PIECE, PARTS)

        @pl.when((step >= HAND_LAG) & (step < SHIFTS + HAND_LAG))
        def _():
            k = step - HAND_LAG
            await_bytes(rows.at[core, span(3 * SHIFTS + k, PIECE)], f_recv.at[k])
            c_copy(3 * SHIFTS + k, PIECE, PARTS)

        @pl.when((step % 2 == 1) & (step < STEPS_SEND - 2))
        def _():
            group = AHEAD // SIDE + (step + 1) // 2
            collect(group)

            @pl.when(group == SIDE)
            def _():
                own_piece(SHIFTS)
                c_copy(SHIFTS)

        pl.when(first >= 0)(functools.partial(finish, first))

        @pl.when(second >= 0)
        def _():
            begin(second)
            finish(second)

        @pl.when(step == SHIFTS // 2)
        def _():
            await_bytes(tally_in.at[pl.ds(1, SHIFTS - 1)], t_sem.at[1])
            total = tally[...]
            for k in range(1, SHIFTS):
                total += tally_in[k]
            tally_in[0] = total
            u_copy().start()

    u_copy().wait()
    total = tally_in[0] + tally_other[...]
    named = lax.broadcasted_iota(jnp.int32, total.shape, 0)
    counts = jnp.sum(jnp.where(named == dp, total, 0.0), axis=0, keepdims=True)[:, :1]
    for i in range(4):
        out_ref[i : i + 1, :] = jnp.sum(mom[i], axis=0, keepdims=True)
    out_ref[4:, :] = jnp.broadcast_to(counts, (4, columns))

    await_bytes(outbox.at[pl.ds(0, (SHIFTS - 1) * CAP)], a_send.at[0])
    await_bytes(tally_in.at[pl.ds(1, SHIFTS - 1)], t_sem.at[0])
    await_bytes(rows.at[0, pl.ds(0, SHIFTS * PIECE)], x_send.at[0])
    await_bytes(rows.at[0, pl.ds(0, SHIFTS * PIECE)], f_send.at[0])
    await_bytes(rows.at[0], c_send.at[0])


def refit_columns(sums):
    square, first_moment, cross_term, target, counts = (sums[i] for i in range(5))
    denominator = counts + RIDGE
    diagonal = square + RIDGE
    anchored = cross_term + RIDGE
    determinant = diagonal * denominator - first_moment * first_moment
    refit_scale = (denominator * anchored - first_moment * target) / determinant
    refit_bias = (diagonal * target - first_moment * anchored) / determinant
    return refit_scale[None, None], refit_bias[None, None]


def local(tokens, routes, weight, quantized):
    token_total, width = tokens.shape
    columns = weight.shape[-1]
    vmem = pl.BlockSpec(memory_space=pltpu.VMEM)
    hbm = pl.BlockSpec(memory_space=pl.ANY)
    sems = pltpu.SemaphoreType.DMA
    sums = pl.pallas_call(
        kernel,
        out_shape=jax.ShapeDtypeStruct((8, columns), jnp.float32),
        in_specs=[hbm, hbm, hbm, hbm],
        out_specs=vmem,
        scratch_shapes=[
            pltpu.VMEM(routes.T.shape, jnp.int32),
            pltpu.VMEM((token_total, width // 2), jnp.bfloat16),
            pltpu.VMEM((2, width // 2, 2 * columns), jnp.bfloat16),
            pltpu.VMEM((SHIFTS * CAP, width // 2), jnp.bfloat16),
            pltpu.VMEM((2, 2 * SHIFTS * CAP, width // 2), jnp.bfloat16),
            pltpu.VMEM((SHIFTS, token_total), jnp.float32),
            pltpu.VMEM((GROUP, 2 * columns), jnp.float32),
            pltpu.VMEM((4, 8, columns), jnp.float32),
            pltpu.VMEM((SHIFTS, 128), jnp.float32),
            pltpu.VMEM((SHIFTS, SHIFTS, 128), jnp.float32),
            pltpu.VMEM((SHIFTS, 128), jnp.float32),
            sems((3,)),
            sems((1,)),
            sems((SHIFTS + SHIFTS // 2,)),
            sems((1,)),
            sems((2 * SHIFTS,)),
            sems((1,)),
            sems((SHIFTS,)),
            sems((1,)),
            sems((SHIFTS,)),
            sems((2,)),
            sems((2,)),
        ],
        compiler_params=pltpu.CompilerParams(
            collective_id=0, has_side_effects=True, vmem_limit_bytes=56 << 20
        ),
        cost_estimate=pl.CostEstimate(
            flops=2 * 2048 * 4096 * 768, bytes_accessed=10 << 20, transcendentals=0
        ),
    )(tokens, routes.T, weight, quantized)
    return refit_columns(sums)


def solution(mesh):
    placed = (
        P(("dp", "section"), None),
        P(("dp", "section"), None),
        P("section", "dp", None, "mp"),
        P("section", "dp", None, "mp"),
    )
    return jax.shard_map(
        local,
        mesh=mesh,
        in_specs=placed,
        out_specs=(P("section", "dp", "mp"), P("section", "dp", "mp")),
        check_vma=False,
    )
```
